32 devices in a mesh: proj: 8 (over y, x, core), row: 4 (over z).
Axes of the slice: x: 2, y: 2, z: 4, core: 2. Of those that a mesh axis runs over, the one named last changes fastest.
Arguments:
- projections: float32 [4096, 4, 1536], P('proj', 'row'), may hold values from -40000 to 40000
Outputs:
- gram: float32 [4096, 4096], P('proj', 'row')
The draws below stay inside these ranges and needn't reach their ends.
All inputs are finite; a program needn't handle non-finite values.
Results may differ from the reference program's by a relative error of at most 0.0017.
Values may be sent and summed in bfloat16 or wider, within the bound.
No kernel may reach another device: no remote copies, remote signals or barrier semaphores. Data moves between devices by JAX's collectives and lax.ppermute only.
A program may use at most 128 MiB of HBM per device.

```python
import math
import jax
import jax.numpy as jnp
from jax import lax

PB = 512
COLS = 1536
BAND = 4
NP = 4096


def draw_projections(key, part):
    keys = jax.random.split(jax.random.fold_in(key, 71), 8)
    field_count = 256
    entries = BAND * COLS
    noise = jnp.clip(jax.random.normal(keys[0], (NP, BAND, COLS), jnp.float32), -6.0, 6.0)
    spectrum = 1.0 / jnp.sqrt(1.0 + jnp.arange(field_count, dtype=jnp.float32) / 32.0)
    fields = jnp.clip(jax.random.normal(keys[1], (field_count, entries), jnp.float32), -6.0, 6.0)
    coefs = jnp.clip(jax.random.normal(keys[2], (NP, field_count), jnp.float32), -4.0, 4.0) * spectrum[None, :]
    shared = jnp.dot(coefs, fields, precision=jax.lax.Precision.HIGHEST) / jnp.sqrt(jnp.sum(spectrum * spectrum))
    shared = jnp.clip(shared, -8.0, 8.0).reshape(NP, BAND, COLS)
    mixed = 0.8 * noise + shared
    column_gain = jnp.exp(jax.random.uniform(keys[5], (COLS,), jnp.float32, 0.0, 2.302585))
    row_gain = jnp.exp(2.302585 * jnp.arange(BAND, dtype=jnp.float32) / max(BAND - 1, 1))
    offsets = jax.random.uniform(keys[6], (NP, BAND), jnp.float32, -3.0, 3.0)
    amplitude = jnp.exp(jax.random.uniform(keys[7], (NP,), jnp.float32, -0.693147, 1.609438))
    shaped = mixed * column_gain[None, None, :] + offsets[:, :, None]
    return (shaped * row_gain[None, :, None] * amplitude[:, None, None]).astype(jnp.float32)


def setup_inputs(seed: int = 0) -> dict:
    seeds = jax.random.split(jax.random.key(seed), 2)
    return {
        "projections": draw_projections(jax.random.fold_in(seeds[1], 71), 0),
    }


def reference(projections):
    filtered = projections - lax.optimization_barrier(jnp.mean(projections, axis=2, keepdims=True))
    entries = filtered.shape[1] * filtered.shape[2]
    band_power = lax.optimization_barrier(jnp.sum(filtered * filtered, axis=(1, 2))) / entries
    normed = (filtered * lax.rsqrt(band_power + 1e-05)[:, None, None] * (1.0 / math.sqrt(entries))).astype(jnp.bfloat16)
    flattened = normed.reshape(normed.shape[0], entries).astype(jnp.float32)
    blocks = flattened.reshape(NP // PB, PB, entries)

    def one_block(rows):
        return jnp.dot(rows, flattened.T, preferred_element_type=jnp.float32, precision=lax.Precision.HIGHEST)
    return lax.map(one_block, blocks).reshape(NP, NP)
```

```python
import math

import jax
import jax.numpy as jnp
from jax import lax
from jax.sharding import PartitionSpec as P

CHUNKS = 2
AXES = ("proj", "row")


def hop(x, axis, size, mask):
    return lax.ppermute(x, axis, [(i, i ^ mask) for i in range(size)])


def scale_up(share):
    t = jnp.ones_like(share)
    for e in (32, 16, 8, 4, 2, 1):
        small = share < 2.0 ** (-2 * e)
        t = jnp.where(small, t * 2.0**e, t)
        share = jnp.where(small, share * 2.0 ** (2 * e), share)
    return t


def per_device(projections):
    tile, det_rows, columns = projections.shape
    np_, nr = lax.axis_size("proj"), lax.axis_size("row")
    group = np_ // nr
    entries = det_rows * nr * columns
    p, z = lax.axis_index("proj"), lax.axis_index("row")

    filtered = projections - jnp.mean(projections, axis=2, keepdims=True)
    energy = jnp.sum(filtered * filtered, axis=(1, 2))
    parts = [energy] + [hop(energy, "row", nr, d) for d in range(1, nr)]
    while len(parts) > 1:
        parts = [a + b for a, b in zip(parts[::2], parts[1::2])]
    band_power = parts[0] / entries
    t = scale_up(band_power / (band_power + 1e-05))
    factor = lax.rsqrt(band_power + 1e-05)
    normed = (filtered * factor[:, None, None] * (1.0 / math.sqrt(entries)) * t[:, None, None]).astype(jnp.bfloat16)
    own = normed.reshape(tile, det_rows * columns)
    every_t = lax.all_gather(t, "proj", axis=0, tiled=True)
    piece = tile // CHUNKS
    held = {(0, q): own[q * piece : (q + 1) * piece] for q in range(CHUNKS)}

    def gather(k):
        if k == 0:
            return
        bits = [b for b in (1 << i for i in range(nr.bit_length())) if k & b]
        for q in range(CHUNKS):
            b = bits[q % len(bits)]
            held[k, q] = hop(held[k ^ b, q], "proj", np_, b * group)

    def chain(k, block):
        part = lax.dot_general(own, block, (((1,), (1,)), ((), ())), preferred_element_type=jnp.float32)
        total = part
        carry = part
        for stage in range(1, nr):
            pairs = []
            for src in range(np_):
                d = (src // group) ^ k
                if stage - 1 < d:
                    pairs.append((src * nr + stage - 1, src * nr + stage))
                if nr - stage > d:
                    pairs.append((src * nr + nr - stage, src * nr + nr - stage - 1))
            got = lax.ppermute(carry.astype(jnp.float16), AXES, pairs).astype(jnp.float32)
            carry = part + got
            total = total + got
        return total

    for k in sorted(range(nr), key=lambda k: bin(k).count("1")):
        gather(k)
    result = [[None] * CHUNKS for _ in range(group)]
    for k in range(nr):
        mine = (p // group) ^ k == z
        for q in range(CHUNKS):
            for j in range(group):
                block = held[k, q] if j == 0 else hop(held[k, q], "proj", np_, j)
                total = chain(k, block)
                before = result[j][q]
                result[j][q] = total if before is None else jnp.where(mine, total, before)
    blocks = [jnp.concatenate(r, axis=1) for r in result]
    member = p % group
    ordered = []
    for j in range(group):
        b = blocks[j]
        for i in range(1, group):
            b = jnp.where(member == i, blocks[j ^ i], b)
        ordered.append(b)
    out = jnp.concatenate(ordered, axis=1)
    back = 1.0 / t
    width = tile * group
    across = 1.0 / lax.dynamic_slice_in_dim(every_t, z * width, width)
    return out * back[:, None] * across[None, :]


def solution(mesh):
    return jax.shard_map(
        per_device, mesh=mesh, in_specs=(P("proj", "row", None),), out_specs=P("proj", "row"), check_vma=False
    )
```

```python
import math

import jax
import jax.numpy as jnp
from jax import lax
from jax.experimental import pallas as pl
from jax.experimental.pallas import tpu as pltpu
from jax.sharding import PartitionSpec as P

CHUNKS = 2
EXTRA = 16
STEPS = 2
AXES = ("proj", "row")


def hop(x, axis, size, mask):
    return lax.ppermute(x, axis, [(i, i ^ mask) for i in range(size)])


def scale_up(share):
    t = jnp.ones_like(share)
    for e in (32, 16, 8, 4, 2, 1):
        small = share < 2.0 ** (-2 * e)
        t = jnp.where(small, t * 2.0**e, t)
        share = jnp.where(small, share * 2.0 ** (2 * e), share)
    return t


def filtered_rows(x_ref):
    columns = x_ref.shape[2]
    parts = []
    for d in range(x_ref.shape[1]):
        x = x_ref[:, d, :]
        parts.append(x - jnp.sum(x, axis=1, keepdims=True) * (1.0 / columns))
    return parts


def energy_kernel(x_ref, energy_ref):
    total = 0.0
    for f in filtered_rows(x_ref):
        total = total + jnp.sum(f * f, axis=1, keepdims=True)
    energy_ref[...] = jnp.transpose(jnp.broadcast_to(total, (total.shape[0], 128)))[:1, :]


def norm_kernel(entries, x_ref, *refs):
    energies, out_ref = refs[:-1], refs[-1]
    step, _, columns = x_ref.shape
    i = pl.program_id(0)
    tile = step * pl.num_programs(0)
    parts = [e[...] for e in energies]
    while len(parts) > 1:
        parts = [a + b for a, b in zip(parts[::2], parts[1::2])]
    power = parts[0] / entries
    t = scale_up(power / (power + 1e-05))
    factor = jnp.transpose(jnp.broadcast_to(lax.rsqrt(power + 1e-05), (128, step)))[:, :1]
    up = jnp.transpose(jnp.broadcast_to(t, (128, step)))[:, :1]
    here = pl.ds(pl.multiple_of(i * step, 128), step)
    for d, f in enumerate(filtered_rows(x_ref)):
        normed = f * factor * (1.0 / math.sqrt(entries)) * up
        out_ref[here, d * columns : (d + 1) * columns] = normed.astype(jnp.bfloat16)
    last = slice(out_ref.shape[0] - EXTRA, out_ref.shape[0])

    @pl.when(i == 0)
    def _():
        out_ref[last, :] = jnp.zeros((EXTRA, out_ref.shape[1]), jnp.bfloat16)

    out_ref[last, here] = jnp.broadcast_to(t, (EXTRA, step)).astype(jnp.bfloat16)


def normalize(x, nr):
    tile, det_rows, columns = x.shape
    step = tile // STEPS
    width = det_rows * columns
    rows = pl.BlockSpec((step, det_rows, columns), lambda i: (i, 0, 0))
    line = pl.BlockSpec((1, step), lambda i: (0, i))
    vec = jax.ShapeDtypeStruct((1, tile), jnp.float32)
    energy = pl.pallas_call(energy_kernel, grid=(STEPS,), in_specs=[rows], out_specs=line, out_shape=vec)(x)
    parts = [energy] + [hop(energy, "row", nr, d) for d in range(1, nr)]
    return pl.pallas_call(
        lambda *refs: norm_kernel(width * nr, *refs),
        grid=(STEPS,),
        in_specs=[rows] + [line] * nr,
        out_specs=pl.BlockSpec((tile + EXTRA, width), lambda i: (0, 0)),
        out_shape=jax.ShapeDtypeStruct((tile + EXTRA, width), jnp.bfloat16),
    )(x, *parts)


def gate(x, *others):
    return pl.pallas_call(
        lambda *refs: None,
        in_specs=[pl.BlockSpec(memory_space=pl.ANY)] * (1 + len(others)),
        out_specs=pl.BlockSpec(memory_space=pl.ANY),
        out_shape=jax.ShapeDtypeStruct(x.shape, x.dtype),
        input_output_aliases={0: 0},
        compiler_params=pltpu.CompilerParams(vmem_limit_bytes=1 << 16),
        cost_estimate=pl.CostEstimate(flops=0, bytes_accessed=0, transcendentals=0),
    )(x, *others)


def tree(np_, nr, group, k):
    stages = []
    size = 1
    while size < nr:
        pairs = []
        for s in range(np_):
            d = (s // group) ^ k

            def head(g):
                return min(range(g * size, (g + 1) * size), key=lambda i: abs(i - d))

            for g in range(0, nr // size, 2):
                a, b = head(g), head(g + 1)
                if abs(a - d) < abs(b - d):
                    a, b = b, a
                pairs.append((s * nr + a, s * nr + b))
        stages.append(pairs)
        size *= 2
    return stages


def schedule(nr, group):
    piece_time, sum_time, gap = 1.5, 1.0, 0.35
    free, there, sends = {}, {(0, q): 0.0 for q in range(CHUNKS)}, []
    for w in range(1, nr.bit_length()):
        for q in range(CHUNKS):
            for k in range(1, nr):
                bits = [b for b in (1 << i for i in range(nr.bit_length())) if k & b]
                if len(bits) == w:
                    b = bits[q % w]
                    begin = max(free.get(b, 0.0), there[k ^ b, q] + (gap if w > 1 else 0.0))
                    free[b] = begin + piece_time
                    there[k, q] = free[b] + gap
                    sends.append((k, q, b))
    ready = [(0.2 + 0.5 * j, (0, j)) for j in range(group)] + [(there[k, q], (k, q)) for k, q, _ in sends]
    events = [(time, 1, "unit", unit) for time, unit in ready]
    line = 0.0
    for time, unit in sorted(ready):
        line = max(line, time) + sum_time
        for stage in range(nr.bit_length() - 1):
            events.append((line + gap + stage * (sum_time + gap), 2, stage, unit))
    return sends, [e[2:] for e in sorted(events, key=lambda e: e[:2])]


def per_device(projections):
    tile = projections.shape[0]
    np_, nr = lax.axis_size("proj"), lax.axis_size("row")
    group = np_ // nr
    p, z = lax.axis_index("proj"), lax.axis_index("row")
    member = p % group
    piece = tile // CHUNKS
    stages = {k: tree(np_, nr, group, k) for k in range(nr)}
    mine = {k: (p // group) ^ k == z for k in range(nr)}
    sends, events = schedule(nr, group)

    block = normalize(projections, nr)
    own = block[:tile]
    held = {(0, q): block[q * piece : (q + 1) * piece + (EXTRA if q == CHUNKS - 1 else 0)] for q in range(CHUNKS)}

    def forward(src):
        for k, q, b in sends:
            if (k ^ b, q) == src:
                held[k, q] = hop(held[src], "proj", np_, b * group)

    for q in range(CHUNKS):
        forward((0, q))
    siblings = [block] + [hop(block, "proj", np_, j) for j in range(1, group)]

    def product(rows, columns):
        return lax.dot_general(rows, columns, (((1,), (1,)), ((), ())), preferred_element_type=jnp.float32)

    token, everyone = [], None
    carry, moving, result, scale = {}, {}, {}, None
    for kind, unit in events:
        k, q = unit
        if kind == "unit":
            if k == 0:
                if q:
                    siblings[q] = gate(siblings[q], *token)
                carry[unit] = product(siblings[q][:tile], own)
            else:
                if everyone is None:
                    everyone = jnp.concatenate([s[:tile] for s in siblings], axis=0)
                    scale = block[tile : tile + 1, :tile]
                held[unit] = gate(held[unit], *token)
                forward(unit)
                carry[unit] = product(everyone, held[unit][:piece])
                if q == CHUNKS - 1:
                    scale = jnp.where(mine[k], held[unit][piece : piece + 1, :tile], scale)
            message = carry[unit].astype(jnp.float16)
            moving[unit] = lax.ppermute(message, AXES, stages[k][0])
        else:
            carry[unit] = gate(carry[unit], *token) + moving[unit].astype(jnp.float32)
            if kind + 1 < len(stages[k]):
                message = carry[unit].astype(jnp.float16)
                moving[unit] = lax.ppermute(message, AXES, stages[k][kind + 1])
            else:
                if k == 0:
                    now = {(q, i): carry[unit][:, i * piece : (i + 1) * piece] for i in range(CHUNKS)}
                else:
                    now = {(j, q): carry[unit][j * tile : (j + 1) * tile] for j in range(group)}
                for at, r in now.items():
                    result[at] = r if at not in result else jnp.where(mine[k], r, result[at])
        token = [carry[unit]]

    across = 1.0 / scale.astype(jnp.float32)
    parts = []
    for j in range(group):
        r = jnp.concatenate([result[j, i] for i in range(CHUNKS)], axis=1) * across
        parts.append(hop(r, "proj", np_, j) if j else r)
    columns = []
    for j in range(group):
        b = parts[j]
        for i in range(1, group):
            b = jnp.where(member == i, parts[j ^ i], b)
        columns.append(b)
    down = 1.0 / block[tile : tile + 1, :tile].astype(jnp.float32)
    return jnp.concatenate(columns, axis=1) * down.reshape(tile, 1)


def solution(mesh):
    return jax.shard_map(
        per_device, mesh=mesh, in_specs=(P("proj", "row", None),), out_specs=P("proj", "row"), check_vma=False
    )
```

```python
import math

import jax
import jax.numpy as jnp
from jax import lax
from jax.experimental import pallas as pl
from jax.experimental.pallas import tpu as pltpu
from jax.sharding import PartitionSpec as P

EXTRA = 16
BITS = (32, 16, 8, 4, 2, 1)
CHUNKS = 2
STEPS = 2
AXES = ("proj", "row")
ROWS = {"x": "own", "y": "own"}
EVENTS = (
    ("hop", ("x", 0), 0),
    ("hop", ("own", 0), 0),
    ("hop", ("y", 0), 0),
    ("begin", ("oo", 0), 0),
    ("hop", ("x", 1), 1),
    ("hop", ("y", 1), 1),
    ("begin", ("os", 0), 1),
    ("first", ("oo", 0), 1),
    ("begin", ("x", 0), 1),
    ("begin", ("y", 0), 1),
    ("second", ("oo", 0), 1),
    ("begin", ("x", 1), 1),
    ("begin", ("y", 1), 1),
    ("first", ("os", 0), 1),
    ("begin", ("xy", 0), 1),
    ("first", ("x", 1), 1),
    ("first", ("x", 0), 1),
    ("first", ("y", 0), 1),
    ("first", ("y", 1), 1),
    ("first", ("xy", 0), 1),
    ("second", ("os", 0), 1),
    ("second", ("x", 0), 1),
    ("second", ("y", 0), 1),
    ("second", ("x", 1), 1),
    ("second", ("y", 1), 1),
    ("send", ("y", 0), 1),
    ("send", ("x", 0), 1),
    ("second", ("xy", 0), 1),
    ("wait", ("x", 0), 1),
    ("wait", ("y", 0), 1),
    ("send", ("plain", 0), 1),
    ("send", ("mirror", 0), 0),
)


def hop(x, axis, size, mask):
    return lax.ppermute(x, axis, [(i, i ^ mask) for i in range(size)])


def exponent_up(share):
    e = jnp.zeros_like(share)
    for b in BITS:
        small = share < 2.0 ** (-2 * b)
        e = jnp.where(small, e + b, e)
        share = jnp.where(small, share * 2.0 ** (2 * b), share)
    return e


def power_of_two(e, sign):
    t = jnp.ones_like(e)
    for b in BITS:
        hit = e >= b
        t = jnp.where(hit, t * 2.0 ** (sign * b), t)
        e = jnp.where(hit, e - b, e)
    return t


def column(row):
    return jnp.transpose(jnp.broadcast_to(row, (128, row.shape[1])))[:, :1]


def energy_kernel(x_ref, energy_ref):
    x = x_ref[:, 0, :]
    f = x - jnp.sum(x, axis=1, keepdims=True) * (1.0 / x.shape[1])
    total = jnp.sum(f * f, axis=1, keepdims=True)
    energy_ref[...] = jnp.transpose(jnp.broadcast_to(total, (total.shape[0], 128)))[:1, :]


def norm_kernel(entries, x_ref, *refs):
    energies, (own_ref, e_ref), piece_refs = refs[: -2 - CHUNKS], refs[-2 - CHUNKS : -CHUNKS], refs[-CHUNKS:]
    step, _, columns = x_ref.shape
    i = pl.program_id(0)
    parts = [e[...] for e in energies]
    while len(parts) > 1:
        parts = [a + b for a, b in zip(parts[::2], parts[1::2])]
    power = parts[0] / entries
    e = exponent_up(power / (power + 1e-05))
    up = column(power_of_two(e, 1))
    factor = column(lax.rsqrt(power + 1e-05))
    x = x_ref[:, 0, :]
    f = x - jnp.sum(x, axis=1, keepdims=True) * (1.0 / columns)
    normed = (f * factor * (1.0 / math.sqrt(entries)) * up).astype(jnp.bfloat16)
    own_ref[...] = normed
    e_ref[...] = e
    for q in range(CHUNKS):

        @pl.when(i == q)
        def _(q=q):
            piece_refs[q][:step, :] = normed

    last = slice(step, step + EXTRA)

    @pl.when(i == 0)
    def _():
        piece_refs[-1][last, :] = jnp.zeros((EXTRA, columns), jnp.bfloat16)

    here = pl.ds(pl.multiple_of(i * step, 128), step)
    piece_refs[-1][last, here] = jnp.broadcast_to(e, (EXTRA, step)).astype(jnp.bfloat16)


def normalize(x, nr):
    tile, _, columns = x.shape
    step = tile // CHUNKS
    rows = pl.BlockSpec((step, 1, columns), lambda i: (i, 0, 0))
    line = pl.BlockSpec((1, step), lambda i: (0, i))
    vec = jax.ShapeDtypeStruct((1, tile), jnp.float32)
    energy = pl.pallas_call(energy_kernel, grid=(CHUNKS,), in_specs=[rows], out_specs=line, out_shape=vec)(x)
    parts = [energy] + [hop(energy, "row", nr, d) for d in range(1, nr)]
    sizes = [step] * (CHUNKS - 1) + [step + EXTRA]
    return pl.pallas_call(
        lambda *refs: norm_kernel(columns * nr, *refs),
        grid=(CHUNKS,),
        in_specs=[rows] + [line] * nr,
        out_specs=[pl.BlockSpec((step, columns), lambda i: (i, 0)), line]
        + [pl.BlockSpec((n, columns), lambda i: (0, 0)) for n in sizes],
        out_shape=[jax.ShapeDtypeStruct((tile, columns), jnp.bfloat16), vec]
        + [jax.ShapeDtypeStruct((n, columns), jnp.bfloat16) for n in sizes],
    )(x, *parts)


def gate(x, *others):
    return pl.pallas_call(
        lambda *refs: None,
        in_specs=[pl.BlockSpec(memory_space=pl.ANY)] * (1 + len(others)),
        out_specs=pl.BlockSpec(memory_space=pl.ANY),
        out_shape=jax.ShapeDtypeStruct(x.shape, x.dtype),
        input_output_aliases={0: 0},
        compiler_params=pltpu.CompilerParams(vmem_limit_bytes=1 << 16),
        cost_estimate=pl.CostEstimate(flops=0, bytes_accessed=0, transcendentals=0),
    )(x, *others)


def arrived(x):
    return x[:8, :128].astype(jnp.float32)


def tree(np_, nr, group, k):
    stages = []
    size = 1
    while size < nr:
        pairs = []
        for s in range(np_):
            d = (s // group) ^ k

            def head(g):
                return min(range(g * size, (g + 1) * size), key=lambda i: abs(i - d))

            for g in range(0, nr // size, 2):
                a, b = head(g), head(g + 1)
                if abs(a - d) < abs(b - d):
                    a, b = b, a
                pairs.append((s * nr + a, s * nr + b))
        stages.append(pairs)
        size *= 2
    return stages


def assemble_kernel(place_ref, own_ref, first_e_ref, second_e_ref, first_ref, second_ref, turned_ref, out_ref):
    tile = first_ref.shape[1]
    down = column(power_of_two(own_ref[...], -1))
    first = first_ref[...] * down * power_of_two(first_e_ref[...], -1)
    second = (second_ref[...] + jnp.transpose(turned_ref[...])) * down * power_of_two(second_e_ref[...], -1)
    at = place_ref[0] == 0

    @pl.when(at)
    def _():
        out_ref[:, :tile] = first
        out_ref[:, tile:] = second

    @pl.when(jnp.logical_not(at))
    def _():
        out_ref[:, :tile] = second
        out_ref[:, tile:] = first


def assemble(place, e_own, e_first, e_second, first, second, turned):
    tile = first.shape[0]
    step = tile // STEPS
    line = pl.BlockSpec((1, tile), lambda i: (0, 0))
    rows = pl.BlockSpec((step, tile), lambda i: (i, 0))
    return pl.pallas_call(
        assemble_kernel,
        grid=(STEPS,),
        in_specs=[
            pl.BlockSpec(memory_space=pltpu.SMEM),
            pl.BlockSpec((1, step), lambda i: (0, i)),
            line,
            line,
            rows,
            rows,
            pl.BlockSpec((tile, step), lambda i: (0, i)),
        ],
        out_specs=pl.BlockSpec((step, 2 * tile), lambda i: (i, 0)),
        out_shape=jax.ShapeDtypeStruct((tile, 2 * tile), jnp.float32),
    )(place, e_own, e_first, e_second, first, second, turned)


def product(rows, columns):
    return lax.dot_general(rows, columns, (((1,), (1,)), ((), ())), preferred_element_type=jnp.float32)


def paired(projections):
    tile, _, columns = projections.shape
    np_, nr = lax.axis_size("proj"), lax.axis_size("row")
    p, z = lax.axis_index("proj"), lax.axis_index("row")
    c, h = p // 2, p % 2
    x, y = c % 2, c // 2
    k = c ^ z
    chips = range(np_ // 2)
    half, piece = tile // 2, tile // CHUNKS

    def receive(value, source):
        pairs = []
        for c in chips:
            for h in range(2):
                for z in range(nr):
                    at = source(c, h, z)
                    if at is not None:
                        pairs.append(((2 * at[0] + at[1]) * nr + at[2], (2 * c + h) * nr + z))
        return lax.ppermute(value, AXES, pairs)

    stages = {n: tree(np_, nr, 2, m) for n, m in (("oo", 0), ("os", 0), ("x", 1), ("y", 2))}
    one, two = [], []
    for s in range(np_):
        if s // 2 in (0, nr - 1):
            a, b = [(0, 1), (3, 2)], [(1, 2), (2, 1)]
        else:
            a, b = [(0, 1), (1, 0), (2, 3), (3, 2)], [(1, 3), (2, 0)]
        one += [(s * nr + i, s * nr + j) for i, j in a]
        two += [(s * nr + i, s * nr + j) for i, j in b]
    stages["xy"] = [one, two]

    carry, moving, token = {}, {}, []

    def ordered(value, wait):
        return gate(value, *token) if token and wait else value

    def send(name, stage):
        moving[name] = lax.ppermute(carry[name].astype(jnp.float16), AXES, stages[name[0]][stage])
        token[:] = [carry[name]]

    def begin(name, part):
        carry[name] = part
        send(name, 0)

    def exponents(b):
        return b[b.shape[0] - EXTRA : b.shape[0] - EXTRA + 1, :tile].astype(jnp.float32)

    own, e_own, *pieces = normalize(projections, nr)
    def from_x(c, h, z):
        return c ^ 1, h ^ (c & 1), z

    def from_y(c, h, z):
        return c ^ 2, h ^ (c & 1) ^ (c >> 1), z

    def whole(axis):
        return jnp.concatenate([got[axis, i][:piece] for i in range(CHUNKS)], axis=0)

    def wide(axis):
        return jnp.concatenate([carry[axis, i] for i in range(CHUNKS)], axis=1)

    def message(total, e):
        below = jnp.broadcast_to(ordered(e, wait), (EXTRA, tile))
        return jnp.concatenate([total.astype(jnp.float16), below.astype(jnp.float16)], axis=0)

    got, rows, arrived = {}, {"own": own}, {}
    for kind, name, wait in EVENTS:
        what, i = name
        if kind == "hop":
            if what == "own":
                sibling = hop(ordered(own, wait), "proj", np_, 1)
            else:
                got[name] = receive(ordered(pieces[i], wait), from_x if what == "x" else from_y)
        elif kind == "begin":
            if what == "oo":
                begin(name, product(own, own))
            elif what == "os":
                sibling = ordered(sibling, wait)
                rows["both"] = jnp.concatenate([own, sibling], axis=0)
                begin(name, jnp.where(h == 0, product(own[:half], sibling), product(sibling[half:], own)))
            elif what == "xy":
                begin(name, product(ordered(whole("x"), wait), whole("y")))
            else:
                got[name] = ordered(got[name], wait)
                begin(name, product(rows[ROWS[what]], got[name][:piece]))
        elif kind == "first":
            carry[name] = ordered(carry[name], wait) + moving[name].astype(jnp.float32)
            send(name, 1)
        elif kind == "second":
            carry[name] = ordered(carry[name], wait) + moving[name].astype(jnp.float32)
            token[:] = [carry[name]]
        elif kind == "wait":
            token.append(arrived[what][:8, :128].astype(jnp.float32))
        elif what == "plain":
            arrived[what] = receive(
                message(carry["xy", 0], exponents(got["y", CHUNKS - 1])),
                lambda c, h, z: (c ^ 1, h ^ (c & 1) ^ 1, z) if c ^ z == 3 else None,
            )
        elif what == "mirror":
            arrived[what] = receive(
                message(carry["xy", 0], exponents(got["x", CHUNKS - 1])),
                lambda c, h, z: (c ^ 2, h ^ (c & 1) ^ (c >> 1) ^ 1, z) if c ^ z == 3 else None,
            )
        elif what == "x":
            arrived[what] = receive(
                message(wide("x"), e_own), lambda c, h, z: (c ^ 1, h ^ (c & 1) ^ 1, c) if c ^ z == 1 else None
            )
        elif what == "y":
            arrived[what] = receive(
                message(wide("y"), e_own),
                lambda c, h, z: (c ^ 2, h ^ (c & 1) ^ (c >> 1) ^ 1, c) if c ^ z == 2 else None,
            )

    wide = {a: wide(a) for a in "xy"}
    plain, mirror = arrived["plain"], arrived["mirror"]
    e_x, e_y = exponents(got["x", CHUNKS - 1]), exponents(got["y", CHUNKS - 1])
    pad = jnp.concatenate([carry["os", 0], jnp.broadcast_to(e_own, (half, tile))], axis=0)
    if ROWS == {"x": "own", "y": "own"}:
        other = hop(pad, "proj", np_, 1)
    else:
        sent = {a: wide[a][tile:] * power_of_two(e, -1) if ROWS[a] == "both" else jnp.zeros_like(pad) for a, e in (("x", e_x), ("y", e_y))}
        other = hop(jnp.where(k == 0, pad, jnp.where(k == 1, sent["x"], sent["y"])), "proj", np_, 1)
    zero = jnp.zeros((tile, tile), jnp.float32)
    straight = jnp.where(k == 0, carry["oo", 0], jnp.where(k == 1, wide["x"][:tile], jnp.where(k == 2, wide["y"][:tile], zero)))
    straight = straight + plain[:tile].astype(jnp.float32)
    low, high = jnp.where(h == 0, carry["os", 0], other[:half]), jnp.where(h == 0, other[:half], carry["os", 0])
    cross = jnp.concatenate([low, high], axis=0)
    from_sibling = jnp.zeros_like(k == 0)
    for a, m in (("x", 1), ("y", 2)):
        if ROWS[a] == "both":
            from_sibling = from_sibling | (k == m)
    second = jnp.where(k == 0, jnp.where(h == 0, cross, zero), jnp.where(from_sibling, other, zero))
    turned = jnp.where((k == 0) & (h == 1), cross, zero) + mirror[:tile].astype(jnp.float32)
    e_first = jnp.where(k == 0, e_own, jnp.where(k == 1, e_x, jnp.where(k == 2, e_y, 0.0))) + exponents(plain)
    e_second = jnp.where(k == 0, other[half : half + 1], 0.0) + exponents(mirror)
    for a in "xy":
        if ROWS[a] == "own":
            turned = turned + arrived[a][:tile].astype(jnp.float32)
            e_second = e_second + exponents(arrived[a])
    place = jnp.where(k == 0, h, jnp.where(k == 1, h ^ x, jnp.where(k == 2, h ^ x ^ y, h ^ y)))
    return assemble(place.reshape(1), e_own, e_first, e_second, straight, second, turned)


def plain_plan(projections):
    tile, det_rows, columns = projections.shape
    entries = det_rows * lax.axis_size("row") * columns
    filtered = projections - jnp.mean(projections, axis=2, keepdims=True)
    power = lax.psum(jnp.sum(filtered * filtered, axis=(1, 2)), "row") / entries
    normed = filtered * lax.rsqrt(power + 1e-05)[:, None, None] * (1.0 / math.sqrt(entries))
    own = normed.astype(jnp.bfloat16).reshape(tile, det_rows * columns)
    part = product(own, lax.all_gather(own, "proj", axis=0, tiled=True))
    return lax.psum_scatter(part, "row", scatter_dimension=1, tiled=True)


def solution(mesh):
    fits = mesh.shape["row"] == 4 and mesh.shape["proj"] == 8
    return jax.shard_map(
        paired if fits else plain_plan,
        mesh=mesh,
        in_specs=(P("proj", "row", None),),
        out_specs=P("proj", "row"),
        check_vma=False,
    )
```

```python
import math

import jax
import jax.numpy as jnp
from jax import lax
from jax.experimental import pallas as pl
from jax.experimental.pallas import tpu as pltpu
from jax.sharding import PartitionSpec as P

EXTRA = 16
BITS = (32, 16, 8, 4, 2, 1)
CHUNKS = 2
STEPS = 2
AXES = ("proj", "row")
EVENTS = (
    ("hop", ("x", 0), 0),
    ("hop", ("own", 0), 0),
    ("hop", ("y", 0), 0),
    ("begin", ("oo", 0), 0),
    ("begin", ("os", 0), 1),
    ("first", ("oo", 0), 1),
    ("begin", ("x", 0), 1),
    ("hop", ("x", 1), 1),
    ("begin", ("y", 0), 1),
    ("hop", ("y", 1), 1),
    ("first", ("os", 0), 1),
    ("second", ("oo", 0), 1),
    ("first", ("x", 0), 1),
    ("first", ("y", 0), 1),
    ("second", ("os", 0), 1),
    ("begin", ("x", 1), 1),
    ("begin", ("y", 1), 1),
    ("begin", ("xy", 0), 1),
    ("second", ("x", 0), 1),
    ("second", ("y", 0), 1),
    ("first", ("x", 1), 1),
    ("first", ("y", 1), 1),
    ("first", ("xy", 0), 1),
    ("second", ("x", 1), 1),
    ("second", ("y", 1), 1),
    ("send", ("x", 0), 1),
    ("send", ("y", 0), 1),
    ("second", ("xy", 0), 1),
    ("send", ("plain", 0), 1),
    ("send", ("mirror", 0), 1),
)


def hop(x, axis, size, mask):
    return lax.ppermute(x, axis, [(i, i ^ mask) for i in range(size)])


def exponent_up(share):
    e = jnp.zeros_like(share)
    for b in BITS:
        small = share < 2.0 ** (-2 * b)
        e = jnp.where(small, e + b, e)
        share = jnp.where(small, share * 2.0 ** (2 * b), share)
    return e


def power_of_two(e, sign):
    t = jnp.ones_like(e)
    for b in BITS:
        hit = e >= b
        t = jnp.where(hit, t * 2.0 ** (sign * b), t)
        e = jnp.where(hit, e - b, e)
    return t


def column(row):
    return jnp.transpose(jnp.broadcast_to(row, (128, row.shape[1])))[:, :1]


def energy_kernel(x_ref, energy_ref):
    x = x_ref[:, 0, :]
    f = x - jnp.sum(x, axis=1, keepdims=True) * (1.0 / x.shape[1])
    total = jnp.sum(f * f, axis=1, keepdims=True)
    energy_ref[...] = jnp.transpose(jnp.broadcast_to(total, (total.shape[0], 128)))[:1, :]


def norm_kernel(entries, x_ref, *refs):
    energies, (own_ref, e_ref), piece_refs = refs[: -2 - CHUNKS], refs[-2 - CHUNKS : -CHUNKS], refs[-CHUNKS:]
    step, _, columns = x_ref.shape
    i = pl.program_id(0)
    parts = [e[...] for e in energies]
    while len(parts) > 1:
        parts = [a + b for a, b in zip(parts[::2], parts[1::2])]
    power = parts[0] / entries
    e = exponent_up(power / (power + 1e-05))
    up = column(power_of_two(e, 1))
    factor = column(lax.rsqrt(power + 1e-05))
    x = x_ref[:, 0, :]
    f = x - jnp.sum(x, axis=1, keepdims=True) * (1.0 / columns)
    normed = (f * factor * (1.0 / math.sqrt(entries)) * up).astype(jnp.bfloat16)
    own_ref[...] = normed
    e_ref[...] = e
    for q in range(CHUNKS):

        @pl.when(i == q)
        def _(q=q):
            piece_refs[q][:step, :] = normed

    last = slice(step, step + EXTRA)

    @pl.when(i == 0)
    def _():
        piece_refs[-1][last, :] = jnp.zeros((EXTRA, columns), jnp.bfloat16)

    here = pl.ds(pl.multiple_of(i * step, 128), step)
    piece_refs[-1][last, here] = jnp.broadcast_to(e, (EXTRA, step)).astype(jnp.bfloat16)


def normalize(x, nr):
    tile, _, columns = x.shape
    step = tile // CHUNKS
    rows = pl.BlockSpec((step, 1, columns), lambda i: (i, 0, 0))
    line = pl.BlockSpec((1, step), lambda i: (0, i))
    vec = jax.ShapeDtypeStruct((1, tile), jnp.float32)
    energy = pl.pallas_call(energy_kernel, grid=(CHUNKS,), in_specs=[rows], out_specs=line, out_shape=vec)(x)
    parts = [energy] + [hop(energy, "row", nr, d) for d in range(1, nr)]
    sizes = [step] * (CHUNKS - 1) + [step + EXTRA]
    return pl.pallas_call(
        lambda *refs: norm_kernel(columns * nr, *refs),
        grid=(CHUNKS,),
        in_specs=[rows] + [line] * nr,
        out_specs=[pl.BlockSpec((step, columns), lambda i: (i, 0)), line]
        + [pl.BlockSpec((n, columns), lambda i: (0, 0)) for n in sizes],
        out_shape=[jax.ShapeDtypeStruct((tile, columns), jnp.bfloat16), vec]
        + [jax.ShapeDtypeStruct((n, columns), jnp.bfloat16) for n in sizes],
    )(x, *parts)


def gate(x, *others):
    return pl.pallas_call(
        lambda *refs: None,
        in_specs=[pl.BlockSpec(memory_space=pl.ANY)] * (1 + len(others)),
        out_specs=pl.BlockSpec(memory_space=pl.ANY),
        out_shape=jax.ShapeDtypeStruct(x.shape, x.dtype),
        input_output_aliases={0: 0},
        compiler_params=pltpu.CompilerParams(vmem_limit_bytes=1 << 16),
        cost_estimate=pl.CostEstimate(flops=0, bytes_accessed=0, transcendentals=0),
    )(x, *others)


def arrived(x):
    return x[:8, :128].astype(jnp.float32)


def tree(np_, nr, group, k):
    stages = []
    size = 1
    while size < nr:
        pairs = []
        for s in range(np_):
            d = (s // group) ^ k

            def head(g):
                return min(range(g * size, (g + 1) * size), key=lambda i: abs(i - d))

            for g in range(0, nr // size, 2):
                a, b = head(g), head(g + 1)
                if abs(a - d) < abs(b - d):
                    a, b = b, a
                pairs.append((s * nr + a, s * nr + b))
        stages.append(pairs)
        size *= 2
    return stages


def assemble_kernel(place_ref, own_ref, first_e_ref, second_e_ref, plain_e_ref, mirror_e_ref, *refs):
    first_ref, second_ref, turned_ref, plain_ref, mirror_ref, out_ref = refs
    tile = first_ref.shape[1]
    down = column(power_of_two(own_ref[...], -1))
    e_first, e_second = first_e_ref[...] + plain_e_ref[:1, :], second_e_ref[...] + mirror_e_ref[:1, :]
    first = (first_ref[...] + plain_ref[...]) * down * power_of_two(e_first, -1)
    turned = jnp.transpose(turned_ref[...] + mirror_ref[:tile, :])
    second = (second_ref[...] + turned) * down * power_of_two(e_second, -1)
    at = place_ref[0] == 0

    @pl.when(at)
    def _():
        out_ref[:, :tile] = first
        out_ref[:, tile:] = second

    @pl.when(jnp.logical_not(at))
    def _():
        out_ref[:, :tile] = second
        out_ref[:, tile:] = first


def assemble(place, e_own, e_first, e_second, first, second, turned, plain, mirror):
    tile = first.shape[0]
    step = tile // STEPS
    line = pl.BlockSpec((1, tile), lambda i: (0, 0))
    below = pl.BlockSpec((8, tile), lambda i: (tile // 8, 0))
    rows = pl.BlockSpec((step, tile), lambda i: (i, 0))
    return pl.pallas_call(
        assemble_kernel,
        grid=(STEPS,),
        in_specs=[
            pl.BlockSpec(memory_space=pltpu.SMEM),
            pl.BlockSpec((1, step), lambda i: (0, i)),
            line,
            line,
            below,
            below,
            rows,
            rows,
            pl.BlockSpec((tile, step), lambda i: (0, i)),
            rows,
            pl.BlockSpec((tile + EXTRA, step), lambda i: (0, i)),
        ],
        out_specs=pl.BlockSpec((step, 2 * tile), lambda i: (i, 0)),
        out_shape=jax.ShapeDtypeStruct((tile, 2 * tile), jnp.float32),
    )(place, e_own, e_first, e_second, plain, mirror, first, second, turned, plain, mirror)


def product(rows, columns):
    return lax.dot_general(rows, columns, (((1,), (1,)), ((), ())), preferred_element_type=jnp.float32)


def paired(projections):
    tile, _, columns = projections.shape
    np_, nr = lax.axis_size("proj"), lax.axis_size("row")
    p, z = lax.axis_index("proj"), lax.axis_index("row")
    c, h = p // 2, p % 2
    x, y = c % 2, c // 2
    k = c ^ z
    chips = range(np_ // 2)
    half, piece = tile // 2, tile // CHUNKS

    def receive(value, source):
        pairs = []
        for c in chips:
            for h in range(2):
                for z in range(nr):
                    at = source(c, h, z)
                    if at is not None:
                        pairs.append(((2 * at[0] + at[1]) * nr + at[2], (2 * c + h) * nr + z))
        return lax.ppermute(value, AXES, pairs)

    def pairs_of(line):
        found = []
        for s in range(np_):
            found += [(s * nr + i, s * nr + j) for i, j in line(s // 2)]
        return found

    def y_line(c):
        return [[(1, 0), (3, 2)], [(0, 2), (2, 0)]] if c % 2 == 0 else [[(0, 1), (2, 3)], [(1, 3), (3, 1)]]

    def xy_line(c):
        if c in (0, 3):
            return [[(0, 1), (3, 2)], [(1, 2), (2, 1)]]
        return [[(0, 1), (1, 0), (2, 3), (3, 2)], [(1, 3), (2, 0)]]

    stages = {n: tree(np_, nr, 2, m) for n, m in (("oo", 0), ("os", 0), ("x", 1))}
    for n, line in (("y", y_line), ("xy", xy_line)):
        stages[n] = [pairs_of(lambda c: line(c)[i]) for i in range(2)]

    carry, moving, token = {}, {}, []

    def ordered(value, wait):
        return gate(value, *token) if token and wait else value

    def send(name, stage):
        moving[name] = lax.ppermute(carry[name].astype(jnp.float16), AXES, stages[name[0]][stage])
        token[:] = [carry[name]]

    def begin(name, part):
        carry[name] = part
        send(name, 0)

    def exponents(b):
        return b[b.shape[0] - EXTRA : b.shape[0] - EXTRA + 1, :tile].astype(jnp.float32)

    own, e_own, *pieces = normalize(projections, nr)
    def from_x(c, h, z):
        return c ^ 1, h ^ (c & 1), z

    def from_y(c, h, z):
        return c ^ 2, h ^ (c & 1) ^ (c >> 1), z

    def whole(axis):
        return jnp.concatenate([got[axis, i][:piece] for i in range(CHUNKS)], axis=0)

    def wide(axis):
        return jnp.concatenate([carry[axis, i] for i in range(CHUNKS)], axis=1)

    def message(total, e):
        below = jnp.broadcast_to(ordered(e, wait), (EXTRA, tile))
        return jnp.concatenate([total.astype(jnp.float16), below.astype(jnp.float16)], axis=0)

    got, arrived = {}, {}
    for kind, name, wait in EVENTS:
        what, i = name
        if kind == "hop":
            if what == "own":
                sibling = hop(ordered(own, wait), "proj", np_, 1)
            else:
                got[name] = receive(ordered(pieces[i], wait), from_x if what == "x" else from_y)
        elif kind == "begin":
            if what == "oo":
                begin(name, product(own, own))
            elif what == "os":
                sibling = ordered(sibling, wait)
                begin(name, jnp.where(h == 0, product(own[:half], sibling), product(sibling[half:], own)))
            elif what == "xy":
                begin(name, product(ordered(whole("x"), wait), whole("y")))
            else:
                got[name] = ordered(got[name], wait)
                begin(name, product(own, got[name][:piece]))
        elif kind == "first":
            carry[name] = ordered(carry[name], wait) + moving[name].astype(jnp.float32)
            send(name, 1)
        elif kind == "second":
            carry[name] = ordered(carry[name], wait) + moving[name].astype(jnp.float32)
            token[:] = [carry[name]]
        elif kind == "wait":
            token.append(arrived[what][:8, :128].astype(jnp.float32))
        elif what == "plain":
            arrived[what] = receive(
                message(carry["xy", 0], exponents(got["y", CHUNKS - 1])),
                lambda c, h, z: (c ^ 1, h ^ (c & 1) ^ 1, z) if c ^ z == 3 else None,
            )
        elif what == "mirror":
            arrived[what] = receive(
                message(carry["xy", 0], exponents(got["x", CHUNKS - 1])),
                lambda c, h, z: (c ^ 2, h ^ (c & 1) ^ (c >> 1) ^ 1, z) if c ^ z == 3 else None,
            )
        elif what == "x":
            arrived[what] = receive(
                message(wide("x"), e_own), lambda c, h, z: (c ^ 1, h ^ (c & 1) ^ 1, c) if c ^ z == 1 else None
            )
        elif what == "y":
            arrived[what] = receive(
                message(wide("y"), e_own),
                lambda c, h, z: (c ^ 2, h ^ (c & 1) ^ (c >> 1) ^ 1, z) if c ^ z == 2 else None,
            )

    def is_k(m, value):
        return jnp.where(k == m, value, jnp.zeros_like(value))

    e_x, e_y = exponents(got["x", CHUNKS - 1]), exponents(got["y", CHUNKS - 1])
    diagonal, cross = carry["oo", 0], carry["os", 0]
    e_below = jnp.broadcast_to(e_own, (8, tile))
    other = hop(jnp.concatenate([cross, e_below], axis=0), "proj", np_, 1)
    cross = jnp.where(h == 0, jnp.concatenate([cross, other[:half]], axis=0), jnp.concatenate([other[:half], cross], axis=0))
    cross = is_k(0, cross)
    wide_x, wide_y = arrived["x"].astype(jnp.float32), arrived["y"].astype(jnp.float32)
    first = is_k(0, diagonal) + is_k(1, wide("x")) + is_k(2, wide("y"))
    second = jnp.where(h == 0, cross, jnp.zeros_like(cross))
    turned = jnp.where(h == 1, cross, jnp.zeros_like(cross)) + wide_x[:tile] + wide_y[:tile]
    e_first = is_k(0, e_own) + is_k(1, e_x) + is_k(2, e_y)
    e_second = is_k(0, other[half : half + 1]) + exponents(wide_x) + exponents(wide_y)
    plain, mirror = arrived["plain"].astype(jnp.float32), arrived["mirror"].astype(jnp.float32)
    place = jnp.where(k == 0, h, jnp.where(k == 1, h ^ x, jnp.where(k == 2, h ^ x ^ y, h ^ y)))
    return assemble(place.reshape(1), e_own, e_first, e_second, first, second, turned, plain, mirror)


def plain_plan(projections):
    tile, det_rows, columns = projections.shape
    entries = det_rows * lax.axis_size("row") * columns
    filtered = projections - jnp.mean(projections, axis=2, keepdims=True)
    power = lax.psum(jnp.sum(filtered * filtered, axis=(1, 2)), "row") / entries
    normed = filtered * lax.rsqrt(power + 1e-05)[:, None, None] * (1.0 / math.sqrt(entries))
    own = normed.astype(jnp.bfloat16).reshape(tile, det_rows * columns)
    part = product(own, lax.all_gather(own, "proj", axis=0, tiled=True))
    return lax.psum_scatter(part, "row", scatter_dimension=1, tiled=True)


def solution(mesh):
    fits = mesh.shape["row"] == 4 and mesh.shape["proj"] == 8
    return jax.shard_map(
        paired if fits else plain_plan,
        mesh=mesh,
        in_specs=(P("proj", "row", None),),
        out_specs=P("proj", "row"),
        check_vma=False,
    )
```

```python
import math

import jax
import jax.numpy as jnp
from jax import lax
from jax.experimental import pallas as pl
from jax.experimental.pallas import tpu as pltpu
from jax.sharding import PartitionSpec as P

EXTRA = 16
BITS = (32, 16, 8, 4, 2, 1)
CHUNKS = 2
STEPS = 2
AXES = ("proj", "row")
EVENTS = (
    ("hop", ("x", 0), 0),
    ("hop", ("own", 0), 0),
    ("hop", ("y", 0), 0),
    ("begin", ("oo", 0), 0),
    ("begin", ("os", 0), 1),
    ("first", ("oo", 0), 1),
    ("begin", ("y", 0), 1),
    ("hop", ("y", 1), 2),
    ("first", ("os", 0), 1),
    ("begin", ("x", 0), 1),
    ("hop", ("x", 1), 2),
    ("second", ("oo", 0), 1),
    ("first", ("x", 0), 1),
    ("first", ("y", 0), 1),
    ("begin", ("x", 1), 1),
    ("second", ("os", 0), 1),
    ("begin", ("y", 1), 1),
    ("begin", ("xy", 0), 1),
    ("first", ("x", 1), 1),
    ("second", ("x", 0), 1),
    ("second", ("y", 0), 1),
    ("first", ("y", 1), 1),
    ("first", ("xy", 0), 1),
    ("second", ("x", 1), 1),
    ("second", ("y", 1), 1),
    ("send", ("x", 0), 1),
    ("send", ("y", 0), 1),
    ("second", ("xy", 0), 1),
    ("send", ("plain", 0), 1),
    ("send", ("mirror", 0), 1),
)


def hop(x, axis, size, mask):
    return lax.ppermute(x, axis, [(i, i ^ mask) for i in range(size)])


def exponent_up(share):
    e = jnp.zeros_like(share)
    for b in BITS:
        small = share < 2.0 ** (-2 * b)
        e = jnp.where(small, e + b, e)
        share = jnp.where(small, share * 2.0 ** (2 * b), share)
    return e


def power_of_two(e, sign):
    t = jnp.ones_like(e)
    for b in BITS:
        hit = e >= b
        t = jnp.where(hit, t * 2.0 ** (sign * b), t)
        e = jnp.where(hit, e - b, e)
    return t


def column(row):
    return jnp.transpose(jnp.broadcast_to(row, (128, row.shape[1])))[:, :1]


def energy_kernel(x_ref, energy_ref):
    x = x_ref[:, 0, :]
    f = x - jnp.sum(x, axis=1, keepdims=True) * (1.0 / x.shape[1])
    total = jnp.sum(f * f, axis=1, keepdims=True)
    energy_ref[...] = jnp.transpose(jnp.broadcast_to(total, (total.shape[0], 128)))[:1, :]


def norm_kernel(entries, x_ref, *refs):
    energies, (own_ref, e_ref), piece_refs = refs[: -2 - CHUNKS], refs[-2 - CHUNKS : -CHUNKS], refs[-CHUNKS:]
    step, _, columns = x_ref.shape
    i = pl.program_id(0)
    parts = [e[...] for e in energies]
    while len(parts) > 1:
        parts = [a + b for a, b in zip(parts[::2], parts[1::2])]
    power = parts[0] / entries
    e = exponent_up(power / (power + 1e-05))
    up = column(power_of_two(e, 1))
    factor = column(lax.rsqrt(power + 1e-05))
    x = x_ref[:, 0, :]
    f = x - jnp.sum(x, axis=1, keepdims=True) * (1.0 / columns)
    normed = (f * factor * (1.0 / math.sqrt(entries)) * up).astype(jnp.bfloat16)
    own_ref[...] = normed
    e_ref[...] = e
    for q in range(CHUNKS):

        @pl.when(i == q)
        def _(q=q):
            piece_refs[q][:step, :] = normed

    last = slice(step, step + EXTRA)

    @pl.when(i == 0)
    def _():
        piece_refs[-1][last, :] = jnp.zeros((EXTRA, columns), jnp.bfloat16)

    here = pl.ds(pl.multiple_of(i * step, 128), step)
    piece_refs[-1][last, here] = jnp.broadcast_to(e, (EXTRA, step)).astype(jnp.bfloat16)


def normalize(x, nr):
    tile, _, columns = x.shape
    step = tile // CHUNKS
    rows = pl.BlockSpec((step, 1, columns), lambda i: (i, 0, 0))
    line = pl.BlockSpec((1, step), lambda i: (0, i))
    vec = jax.ShapeDtypeStruct((1, tile), jnp.float32)
    energy = pl.pallas_call(energy_kernel, grid=(CHUNKS,), in_specs=[rows], out_specs=line, out_shape=vec)(x)
    parts = [energy] + [hop(energy, "row", nr, d) for d in range(1, nr)]
    sizes = [step] * (CHUNKS - 1) + [step + EXTRA]
    return pl.pallas_call(
        lambda *refs: norm_kernel(columns * nr, *refs),
        grid=(CHUNKS,),
        in_specs=[rows] + [line] * nr,
        out_specs=[pl.BlockSpec((step, columns), lambda i: (i, 0)), line]
        + [pl.BlockSpec((n, columns), lambda i: (0, 0)) for n in sizes],
        out_shape=[jax.ShapeDtypeStruct((tile, columns), jnp.bfloat16), vec]
        + [jax.ShapeDtypeStruct((n, columns), jnp.bfloat16) for n in sizes],
    )(x, *parts)


def gate(x, *others):
    return pl.pallas_call(
        lambda *refs: None,
        in_specs=[pl.BlockSpec(memory_space=pl.ANY)] * (1 + len(others)),
        out_specs=pl.BlockSpec(memory_space=pl.ANY),
        out_shape=jax.ShapeDtypeStruct(x.shape, x.dtype),
        input_output_aliases={0: 0},
        compiler_params=pltpu.CompilerParams(vmem_limit_bytes=1 << 16),
        cost_estimate=pl.CostEstimate(flops=0, bytes_accessed=0, transcendentals=0),
    )(x, *others)


def arrived(x):
    return x[:8, :128].astype(jnp.float32)


def tree(np_, nr, group, k):
    stages = []
    size = 1
    while size < nr:
        pairs = []
        for s in range(np_):
            d = (s // group) ^ k

            def head(g):
                return min(range(g * size, (g + 1) * size), key=lambda i: abs(i - d))

            for g in range(0, nr // size, 2):
                a, b = head(g), head(g + 1)
                if abs(a - d) < abs(b - d):
                    a, b = b, a
                pairs.append((s * nr + a, s * nr + b))
        stages.append(pairs)
        size *= 2
    return stages


def assemble_kernel(place_ref, own_ref, first_e_ref, second_e_ref, plain_e_ref, mirror_e_ref, *refs):
    first_ref, second_ref, turned_ref, plain_ref, mirror_ref, out_ref = refs
    tile = first_ref.shape[1]
    down = column(power_of_two(own_ref[...], -1))
    e_first, e_second = first_e_ref[...] + plain_e_ref[:1, :], second_e_ref[...] + mirror_e_ref[:1, :]
    first = (first_ref[...] + plain_ref[...]) * down * power_of_two(e_first, -1)
    turned = jnp.transpose(turned_ref[...] + mirror_ref[:tile, :])
    second = (second_ref[...] + turned) * down * power_of_two(e_second, -1)
    at = place_ref[0] == 0

    @pl.when(at)
    def _():
        out_ref[:, :tile] = first
        out_ref[:, tile:] = second

    @pl.when(jnp.logical_not(at))
    def _():
        out_ref[:, :tile] = second
        out_ref[:, tile:] = first


def assemble(place, e_own, e_first, e_second, first, second, turned, plain, mirror):
    tile = first.shape[0]
    step = tile // STEPS
    line = pl.BlockSpec((1, tile), lambda i: (0, 0))
    below = pl.BlockSpec((8, tile), lambda i: (tile // 8, 0))
    rows = pl.BlockSpec((step, tile), lambda i: (i, 0))
    return pl.pallas_call(
        assemble_kernel,
        grid=(STEPS,),
        in_specs=[
            pl.BlockSpec(memory_space=pltpu.SMEM),
            pl.BlockSpec((1, step), lambda i: (0, i)),
            line,
            line,
            below,
            below,
            rows,
            rows,
            pl.BlockSpec((tile, step), lambda i: (0, i)),
            rows,
            pl.BlockSpec((tile + EXTRA, step), lambda i: (0, i)),
        ],
        out_specs=pl.BlockSpec((step, 2 * tile), lambda i: (i, 0)),
        out_shape=jax.ShapeDtypeStruct((tile, 2 * tile), jnp.float32),
    )(place, e_own, e_first, e_second, plain, mirror, first, second, turned, plain, mirror)


def product(rows, columns):
    return lax.dot_general(rows, columns, (((1,), (1,)), ((), ())), preferred_element_type=jnp.float32)


def paired(projections):
    tile, _, columns = projections.shape
    np_, nr = lax.axis_size("proj"), lax.axis_size("row")
    p, z = lax.axis_index("proj"), lax.axis_index("row")
    c, h = p // 2, p % 2
    x, y = c % 2, c // 2
    k = c ^ z
    chips = range(np_ // 2)
    half, piece = tile // 2, tile // CHUNKS

    def receive(value, source):
        pairs = []
        for c in chips:
            for h in range(2):
                for z in range(nr):
                    at = source(c, h, z)
                    if at is not None:
                        pairs.append(((2 * at[0] + at[1]) * nr + at[2], (2 * c + h) * nr + z))
        return lax.ppermute(value, AXES, pairs)

    def pairs_of(line):
        found = []
        for s in range(np_):
            found += [(s * nr + i, s * nr + j) for i, j in line(s // 2)]
        return found

    def y_line(c):
        return [[(1, 0), (3, 2)], [(0, 2), (2, 0)]] if c % 2 == 0 else [[(0, 1), (2, 3)], [(1, 3), (3, 1)]]

    def xy_line(c):
        if c in (0, 3):
            return [[(0, 1), (3, 2)], [(1, 2), (2, 1)]]
        return [[(0, 1), (1, 0), (2, 3), (3, 2)], [(1, 3), (2, 0)]]

    stages = {n: tree(np_, nr, 2, m) for n, m in (("oo", 0), ("os", 0), ("x", 1))}
    for n, line in (("y", y_line), ("xy", xy_line)):
        stages[n] = [pairs_of(lambda c: line(c)[i]) for i in range(2)]

    carry, moving, token = {}, {}, []

    def ordered(value, wait):
        return gate(value, *token) if token and wait else value

    def send(name, stage):
        moving[name] = lax.ppermute(carry[name].astype(jnp.float16), AXES, stages[name[0]][stage])
        token[:] = [carry[name]]

    def begin(name, part):
        carry[name] = part
        send(name, 0)

    def exponents(b):
        return b[b.shape[0] - EXTRA : b.shape[0] - EXTRA + 1, :tile].astype(jnp.float32)

    own, e_own, *pieces = normalize(projections, nr)
    def from_x(c, h, z):
        return c ^ 1, h ^ (c & 1), z

    def from_y(c, h, z):
        return c ^ 2, h ^ (c & 1) ^ (c >> 1), z

    def whole(axis):
        return jnp.concatenate([got[axis, i][:piece] for i in range(CHUNKS)], axis=0)

    def wide(axis):
        return jnp.concatenate([carry[axis, i] for i in range(CHUNKS)], axis=1)

    def message(total, e):
        below = jnp.broadcast_to(ordered(e, wait), (EXTRA, tile))
        return jnp.concatenate([total.astype(jnp.float16), below.astype(jnp.float16)], axis=0)

    got, arrived = {}, {}
    for kind, name, wait in EVENTS:
        what, i = name
        if kind == "hop":
            if what == "own":
                sibling = hop(ordered(own, wait), "proj", np_, 1)
            else:
                value = gate(pieces[i], got[what, i - 1]) if wait == 2 else ordered(pieces[i], wait)
                got[name] = receive(value, from_x if what == "x" else from_y)
        elif kind == "begin":
            if what == "oo":
                begin(name, product(own, own))
            elif what == "os":
                sibling = ordered(sibling, wait)
                begin(name, jnp.where(h == 0, product(own[:half], sibling), product(sibling[half:], own)))
            elif what == "xy":
                begin(name, product(ordered(whole("x"), wait), whole("y")))
            else:
                got[name] = ordered(got[name], wait)
                begin(name, product(own, got[name][:piece]))
        elif kind == "first":
            carry[name] = ordered(carry[name], wait) + moving[name].astype(jnp.float32)
            send(name, 1)
        elif kind == "second":
            carry[name] = ordered(carry[name], wait) + moving[name].astype(jnp.float32)
            token[:] = [carry[name]]
        elif kind == "wait":
            token.append(arrived[what][:8, :128].astype(jnp.float32))
        elif what == "plain":
            arrived[what] = receive(
                message(carry["xy", 0], exponents(got["y", CHUNKS - 1])),
                lambda c, h, z: (c ^ 1, h ^ (c & 1) ^ 1, z) if c ^ z == 3 else None,
            )
        elif what == "mirror":
            arrived[what] = receive(
                message(carry["xy", 0], exponents(got["x", CHUNKS - 1])),
                lambda c, h, z: (c ^ 2, h ^ (c & 1) ^ (c >> 1) ^ 1, z) if c ^ z == 3 else None,
            )
        elif what == "x":
            arrived[what] = receive(
                message(wide("x"), e_own), lambda c, h, z: (c ^ 1, h ^ (c & 1) ^ 1, c) if c ^ z == 1 else None
            )
        elif what == "y":
            arrived[what] = receive(
                message(wide("y"), e_own),
                lambda c, h, z: (c ^ 2, h ^ (c & 1) ^ (c >> 1) ^ 1, z) if c ^ z == 2 else None,
            )

    def is_k(m, value):
        return jnp.where(k == m, value, jnp.zeros_like(value))

    e_x, e_y = exponents(got["x", CHUNKS - 1]), exponents(got["y", CHUNKS - 1])
    diagonal, cross = carry["oo", 0], carry["os", 0]
    e_below = jnp.broadcast_to(e_own, (8, tile))
    other = hop(jnp.concatenate([cross, e_below], axis=0), "proj", np_, 1)
    cross = jnp.where(h == 0, jnp.concatenate([cross, other[:half]], axis=0), jnp.concatenate([other[:half], cross], axis=0))
    cross = is_k(0, cross)
    wide_x, wide_y = arrived["x"].astype(jnp.float32), arrived["y"].astype(jnp.float32)
    first = is_k(0, diagonal) + is_k(1, wide("x")) + is_k(2, wide("y"))
    second = jnp.where(h == 0, cross, jnp.zeros_like(cross))
    turned = jnp.where(h == 1, cross, jnp.zeros_like(cross)) + wide_x[:tile] + wide_y[:tile]
    e_first = is_k(0, e_own) + is_k(1, e_x) + is_k(2, e_y)
    e_second = is_k(0, other[half : half + 1]) + exponents(wide_x) + exponents(wide_y)
    plain, mirror = arrived["plain"].astype(jnp.float32), arrived["mirror"].astype(jnp.float32)
    place = jnp.where(k == 0, h, jnp.where(k == 1, h ^ x, jnp.where(k == 2, h ^ x ^ y, h ^ y)))
    return assemble(place.reshape(1), e_own, e_first, e_second, first, second, turned, plain, mirror)


def plain_plan(projections):
    tile, det_rows, columns = projections.shape
    entries = det_rows * lax.axis_size("row") * columns
    filtered = projections - jnp.mean(projections, axis=2, keepdims=True)
    power = lax.psum(jnp.sum(filtered * filtered, axis=(1, 2)), "row") / entries
    normed = filtered * lax.rsqrt(power + 1e-05)[:, None, None] * (1.0 / math.sqrt(entries))
    own = normed.astype(jnp.bfloat16).reshape(tile, det_rows * columns)
    part = product(own, lax.all_gather(own, "proj", axis=0, tiled=True))
    return lax.psum_scatter(part, "row", scatter_dimension=1, tiled=True)


def per_device(projections):
    tile, det_rows, columns = projections.shape
    fits = lax.axis_size("proj") == 8 and lax.axis_size("row") == 4 and det_rows == 1
    if fits and tile % (128 * CHUNKS) == 0 and columns >= tile:
        return paired(projections)
    return plain_plan(projections)


def solution(mesh):
    return jax.shard_map(
        per_device, mesh=mesh, in_specs=(P("proj", "row", None),), out_specs=P("proj", "row"), check_vma=False
    )
```

```python
import math

import jax
import jax.numpy as jnp
from jax import lax
from jax.experimental import pallas as pl
from jax.experimental.pallas import tpu as pltpu
from jax.sharding import PartitionSpec as P

EXTRA = 16
BITS = (32, 16, 8, 4, 2, 1)
CHUNKS = 2
STEPS = 2
AXES = ("proj", "row")
EVENTS = (
    ("hop", ("x", 0), 0),
    ("hop", ("own", 0), 0),
    ("hop", ("y", 0), 0),
    ("begin", ("oo", 0), 0),
    ("begin", ("os", 0), 1),
    ("first", ("oo", 0), 1),
    ("begin", ("y", 0), 1),
    ("hop", ("y", 1), 2),
    ("first", ("os", 0), 1),
    ("begin", ("x", 0), 1),
    ("hop", ("x", 1), 2),
    ("second", ("oo", 0), 1),
    ("first", ("x", 0), 1),
    ("first", ("y", 0), 1),
    ("begin", ("x", 1), 1),
    ("second", ("os", 0), 1),
    ("begin", ("y", 1), 1),
    ("begin", ("xy", 0), 1),
    ("first", ("x", 1), 1),
    ("second", ("x", 0), 1),
    ("second", ("y", 0), 1),
    ("first", ("y", 1), 1),
    ("first", ("xy", 0), 1),
    ("second", ("x", 1), 1),
    ("second", ("y", 1), 1),
    ("send", ("x", 0), 1),
    ("send", ("y", 0), 1),
    ("second", ("xy", 0), 1),
    ("send", ("plain", 0), 0),
    ("send", ("mirror", 0), 0),
)


def hop(x, axis, size, mask):
    return lax.ppermute(x, axis, [(i, i ^ mask) for i in range(size)])


def exponent_up(share):
    e = jnp.zeros_like(share)
    for b in BITS:
        small = share < 2.0 ** (-2 * b)
        e = jnp.where(small, e + b, e)
        share = jnp.where(small, share * 2.0 ** (2 * b), share)
    return e


def power_of_two(e, sign):
    t = jnp.ones_like(e)
    for b in BITS:
        hit = e >= b
        t = jnp.where(hit, t * 2.0 ** (sign * b), t)
        e = jnp.where(hit, e - b, e)
    return t


def column(row):
    return jnp.transpose(jnp.broadcast_to(row, (128, row.shape[1])))[:, :1]


def energy_kernel(x_ref, energy_ref):
    x = x_ref[:, 0, :]
    f = x - jnp.sum(x, axis=1, keepdims=True) * (1.0 / x.shape[1])
    total = jnp.sum(f * f, axis=1, keepdims=True)
    energy_ref[...] = jnp.transpose(jnp.broadcast_to(total, (total.shape[0], 128)))[:1, :]


def norm_kernel(entries, x_ref, *refs):
    energies, (own_ref, e_ref), piece_refs = refs[: -2 - CHUNKS], refs[-2 - CHUNKS : -CHUNKS], refs[-CHUNKS:]
    step, _, columns = x_ref.shape
    i = pl.program_id(0)
    parts = [e[...] for e in energies]
    while len(parts) > 1:
        parts = [a + b for a, b in zip(parts[::2], parts[1::2])]
    power = parts[0] / entries
    e = exponent_up(power / (power + 1e-05))
    up = column(power_of_two(e, 1))
    factor = column(lax.rsqrt(power + 1e-05))
    x = x_ref[:, 0, :]
    f = x - jnp.sum(x, axis=1, keepdims=True) * (1.0 / columns)
    normed = (f * factor * (1.0 / math.sqrt(entries)) * up).astype(jnp.bfloat16)
    own_ref[...] = normed
    e_ref[...] = e
    for q in range(CHUNKS):

        @pl.when(i == q)
        def _(q=q):
            piece_refs[q][:step, :] = normed

    last = slice(step, step + EXTRA)

    @pl.when(i == 0)
    def _():
        piece_refs[-1][last, :] = jnp.zeros((EXTRA, columns), jnp.bfloat16)

    here = pl.ds(pl.multiple_of(i * step, 128), step)
    piece_refs[-1][last, here] = jnp.broadcast_to(e, (EXTRA, step)).astype(jnp.bfloat16)


def normalize(x, nr):
    tile, _, columns = x.shape
    step = tile // CHUNKS
    rows = pl.BlockSpec((step, 1, columns), lambda i: (i, 0, 0))
    line = pl.BlockSpec((1, step), lambda i: (0, i))
    vec = jax.ShapeDtypeStruct((1, tile), jnp.float32)
    energy = pl.pallas_call(energy_kernel, grid=(CHUNKS,), in_specs=[rows], out_specs=line, out_shape=vec)(x)
    parts = [energy] + [hop(energy, "row", nr, d) for d in range(1, nr)]
    sizes = [step] * (CHUNKS - 1) + [step + EXTRA]
    return pl.pallas_call(
        lambda *refs: norm_kernel(columns * nr, *refs),
        grid=(CHUNKS,),
        in_specs=[rows] + [line] * nr,
        out_specs=[pl.BlockSpec((step, columns), lambda i: (i, 0)), line]
        + [pl.BlockSpec((n, columns), lambda i: (0, 0)) for n in sizes],
        out_shape=[jax.ShapeDtypeStruct((tile, columns), jnp.bfloat16), vec]
        + [jax.ShapeDtypeStruct((n, columns), jnp.bfloat16) for n in sizes],
    )(x, *parts)


def gate(x, *others):
    return pl.pallas_call(
        lambda *refs: None,
        in_specs=[pl.BlockSpec(memory_space=pl.ANY)] * (1 + len(others)),
        out_specs=pl.BlockSpec(memory_space=pl.ANY),
        out_shape=jax.ShapeDtypeStruct(x.shape, x.dtype),
        input_output_aliases={0: 0},
        compiler_params=pltpu.CompilerParams(vmem_limit_bytes=1 << 16),
        cost_estimate=pl.CostEstimate(flops=0, bytes_accessed=0, transcendentals=0),
    )(x, *others)


def arrived(x):
    return x[:8, :128].astype(jnp.float32)


def tree(np_, nr, group, k):
    stages = []
    size = 1
    while size < nr:
        pairs = []
        for s in range(np_):
            d = (s // group) ^ k

            def head(g):
                return min(range(g * size, (g + 1) * size), key=lambda i: abs(i - d))

            for g in range(0, nr // size, 2):
                a, b = head(g), head(g + 1)
                if abs(a - d) < abs(b - d):
                    a, b = b, a
                pairs.append((s * nr + a, s * nr + b))
        stages.append(pairs)
        size *= 2
    return stages


def assemble_kernel(place_ref, own_ref, first_e_ref, second_e_ref, plain_e_ref, mirror_e_ref, *refs):
    first_ref, second_ref, turned_ref, plain_ref, mirror_ref, out_ref = refs
    tile = first_ref.shape[1]
    down = column(power_of_two(own_ref[...], -1))
    e_first, e_second = first_e_ref[...] + plain_e_ref[:1, :], second_e_ref[...] + mirror_e_ref[:1, :]
    first = (first_ref[...] + plain_ref[...]) * down * power_of_two(e_first, -1)
    turned = jnp.transpose(turned_ref[...] + mirror_ref[:tile, :])
    second = (second_ref[...] + turned) * down * power_of_two(e_second, -1)
    at = place_ref[0] == 0

    @pl.when(at)
    def _():
        out_ref[:, :tile] = first
        out_ref[:, tile:] = second

    @pl.when(jnp.logical_not(at))
    def _():
        out_ref[:, :tile] = second
        out_ref[:, tile:] = first


def assemble(place, e_own, e_first, e_second, first, second, turned, plain, mirror):
    tile = first.shape[0]
    step = tile // STEPS
    line = pl.BlockSpec((1, tile), lambda i: (0, 0))
    below = pl.BlockSpec((8, tile), lambda i: (tile // 8, 0))
    rows = pl.BlockSpec((step, tile), lambda i: (i, 0))
    return pl.pallas_call(
        assemble_kernel,
        grid=(STEPS,),
        in_specs=[
            pl.BlockSpec(memory_space=pltpu.SMEM),
            pl.BlockSpec((1, step), lambda i: (0, i)),
            line,
            line,
            below,
            below,
            rows,
            rows,
            pl.BlockSpec((tile, step), lambda i: (0, i)),
            rows,
            pl.BlockSpec((tile + EXTRA, step), lambda i: (0, i)),
        ],
        out_specs=pl.BlockSpec((step, 2 * tile), lambda i: (i, 0)),
        out_shape=jax.ShapeDtypeStruct((tile, 2 * tile), jnp.float32),
    )(place, e_own, e_first, e_second, plain, mirror, first, second, turned, plain, mirror)


def product(rows, columns):
    return lax.dot_general(rows, columns, (((1,), (1,)), ((), ())), preferred_element_type=jnp.float32)


def paired(projections):
    tile, _, columns = projections.shape
    np_, nr = lax.axis_size("proj"), lax.axis_size("row")
    p, z = lax.axis_index("proj"), lax.axis_index("row")
    c, h = p // 2, p % 2
    x, y = c % 2, c // 2
    k = c ^ z
    chips = range(np_ // 2)
    half, piece = tile // 2, tile // CHUNKS

    def receive(value, source):
        pairs = []
        for c in chips:
            for h in range(2):
                for z in range(nr):
                    at = source(c, h, z)
                    if at is not None:
                        pairs.append(((2 * at[0] + at[1]) * nr + at[2], (2 * c + h) * nr + z))
        return lax.ppermute(value, AXES, pairs)

    def pairs_of(line):
        found = []
        for s in range(np_):
            found += [(s * nr + i, s * nr + j) for i, j in line(s // 2)]
        return found

    def y_line(c):
        return [[(1, 0), (3, 2)], [(0, 2), (2, 0)]] if c % 2 == 0 else [[(0, 1), (2, 3)], [(1, 3), (3, 1)]]

    def xy_line(c):
        if c in (0, 3):
            return [[(0, 1), (3, 2)], [(1, 2), (2, 1)]]
        return [[(0, 1), (1, 0), (2, 3), (3, 2)], [(1, 3), (2, 0)]]

    stages = {n: tree(np_, nr, 2, m) for n, m in (("oo", 0), ("os", 0), ("x", 1))}
    for n, line in (("y", y_line), ("xy", xy_line)):
        stages[n] = [pairs_of(lambda c: line(c)[i]) for i in range(2)]

    carry, moving, token = {}, {}, []

    def ordered(value, wait):
        return gate(value, *token) if token and wait else value

    def send(name, stage):
        moving[name] = lax.ppermute(carry[name].astype(jnp.float16), AXES, stages[name[0]][stage])
        token[:] = [carry[name]]

    def begin(name, part):
        carry[name] = part
        send(name, 0)

    def exponents(b):
        return b[b.shape[0] - EXTRA : b.shape[0] - EXTRA + 1, :tile].astype(jnp.float32)

    own, e_own, *pieces = normalize(projections, nr)
    def from_x(c, h, z):
        return c ^ 1, h ^ (c & 1), z

    def from_y(c, h, z):
        return c ^ 2, h ^ (c & 1) ^ (c >> 1), z

    def whole(axis):
        return jnp.concatenate([got[axis, i][:piece] for i in range(CHUNKS)], axis=0)

    def wide(axis):
        return jnp.concatenate([carry[axis, i] for i in range(CHUNKS)], axis=1)

    def message(total, e):
        below = jnp.broadcast_to(ordered(e, wait), (EXTRA, tile))
        return jnp.concatenate([total.astype(jnp.float16), below.astype(jnp.float16)], axis=0)

    got, arrived = {}, {}
    for kind, name, wait in EVENTS:
        what, i = name
        if kind == "hop":
            if what == "own":
                sibling = hop(ordered(own, wait), "proj", np_, 1)
            else:
                value = gate(pieces[i], got[what, i - 1]) if wait == 2 else ordered(pieces[i], wait)
                got[name] = receive(value, from_x if what == "x" else from_y)
        elif kind == "begin":
            if what == "oo":
                begin(name, product(own, own))
            elif what == "os":
                sibling = ordered(sibling, wait)
                begin(name, jnp.where(h == 0, product(own[:half], sibling), product(sibling[half:], own)))
            elif what == "xy":
                begin(name, product(ordered(whole("x"), wait), whole("y")))
            else:
                got[name] = ordered(got[name], wait)
                begin(name, product(own, got[name][:piece]))
        elif kind == "first":
            carry[name] = ordered(carry[name], wait) + moving[name].astype(jnp.float32)
            send(name, 1)
        elif kind == "second":
            carry[name] = ordered(carry[name], wait) + moving[name].astype(jnp.float32)
            token[:] = [carry[name]]
        elif kind == "wait":
            token.append(arrived[what][:8, :128].astype(jnp.float32))
        elif what == "plain":
            arrived[what] = receive(
                message(carry["xy", 0], exponents(got["y", CHUNKS - 1])),
                lambda c, h, z: (c ^ 1, h ^ (c & 1) ^ 1, z) if c ^ z == 3 else None,
            )
        elif what == "mirror":
            arrived[what] = receive(
                message(carry["xy", 0], exponents(got["x", CHUNKS - 1])),
                lambda c, h, z: (c ^ 2, h ^ (c & 1) ^ (c >> 1) ^ 1, z) if c ^ z == 3 else None,
            )
        elif what == "x":
            arrived[what] = receive(
                message(wide("x"), e_own), lambda c, h, z: (c ^ 1, h ^ (c & 1) ^ 1, c) if c ^ z == 1 else None
            )
        elif what == "y":
            arrived[what] = receive(
                message(wide("y"), e_own),
                lambda c, h, z: (c ^ 2, h ^ (c & 1) ^ (c >> 1) ^ 1, z) if c ^ z == 2 else None,
            )

    def is_k(m, value):
        return jnp.where(k == m, value, jnp.zeros_like(value))

    e_x, e_y = exponents(got["x", CHUNKS - 1]), exponents(got["y", CHUNKS - 1])
    diagonal, cross = carry["oo", 0], carry["os", 0]
    e_below = jnp.broadcast_to(e_own, (8, tile))
    other = hop(jnp.concatenate([cross, e_below], axis=0), "proj", np_, 1)
    cross = jnp.where(h == 0, jnp.concatenate([cross, other[:half]], axis=0), jnp.concatenate([other[:half], cross], axis=0))
    cross = is_k(0, cross)
    wide_x, wide_y = arrived["x"].astype(jnp.float32), arrived["y"].astype(jnp.float32)
    first = is_k(0, diagonal) + is_k(1, wide("x")) + is_k(2, wide("y"))
    second = jnp.where(h == 0, cross, jnp.zeros_like(cross))
    turned = jnp.where(h == 1, cross, jnp.zeros_like(cross)) + wide_x[:tile] + wide_y[:tile]
    e_first = is_k(0, e_own) + is_k(1, e_x) + is_k(2, e_y)
    e_second = is_k(0, other[half : half + 1]) + exponents(wide_x) + exponents(wide_y)
    plain, mirror = arrived["plain"].astype(jnp.float32), arrived["mirror"].astype(jnp.float32)
    place = jnp.where(k == 0, h, jnp.where(k == 1, h ^ x, jnp.where(k == 2, h ^ x ^ y, h ^ y)))
    return assemble(place.reshape(1), e_own, e_first, e_second, first, second, turned, plain, mirror)


def plain_plan(projections):
    tile, det_rows, columns = projections.shape
    entries = det_rows * lax.axis_size("row") * columns
    filtered = projections - jnp.mean(projections, axis=2, keepdims=True)
    power = lax.psum(jnp.sum(filtered * filtered, axis=(1, 2)), "row") / entries
    normed = filtered * lax.rsqrt(power + 1e-05)[:, None, None] * (1.0 / math.sqrt(entries))
    own = normed.astype(jnp.bfloat16).reshape(tile, det_rows * columns)
    part = product(own, lax.all_gather(own, "proj", axis=0, tiled=True))
    return lax.psum_scatter(part, "row", scatter_dimension=1, tiled=True)


def per_device(projections):
    tile, det_rows, columns = projections.shape
    fits = lax.axis_size("proj") == 8 and lax.axis_size("row") == 4 and det_rows == 1
    if fits and tile % (128 * CHUNKS) == 0 and columns >= tile:
        return paired(projections)
    return plain_plan(projections)


def solution(mesh):
    return jax.shard_map(
        per_device, mesh=mesh, in_specs=(P("proj", "row", None),), out_specs=P("proj", "row"), check_vma=False
    )
```
